32 devices in a mesh: dp: 4 (over x, core), row: 4 (over z), col: 2 (over y).
Axes of the slice: x: 2, y: 2, z: 4, core: 2. Of those that a mesh axis runs over, the one named last changes fastest.
Arguments:
- activations: float32 [2048, 4096], P('dp', ('row', 'col')), may hold values from -6 to 6
- weight_block: float32 [4096, 15360], P('row', 'col'), may hold values from -0.09375 to 0.09375
- cotangent: float32 [2048, 15360], P(('dp', 'row'), 'col'), may hold values from -6 to 6
Outputs:
- output_act: float32 [2048, 15360], P(('dp', 'row'), 'col')
- input_grad: float32 [2048, 4096], P('dp', ('row', 'col'))
- weight_grad: float32 [4096, 15360], P('row', 'col')
The draws below stay inside these ranges and needn't reach their ends.
All inputs are finite; a program needn't handle non-finite values.
Results may differ from the reference program's by a relative error of at most 0.000088.
Values sent between devices are 32-bit elements; how exact they have to be, the bound alone decides.
No kernel may reach another device: no remote copies, remote signals or barrier semaphores. Data moves between devices by JAX's collectives and lax.ppermute only.
A program may use at most 256 MiB of HBM per device.

```python
import jax
import jax.numpy as jnp
from jax import lax

D = 4096
FF = 15360
TOKENS = 2048


def level_of(own_key, dims, pieces, smallest, largest):
    loudness = 1.0
    for dim, shards_of in pieces:
        draws = jax.random.uniform(jax.random.fold_in(jax.random.fold_in(own_key, 6), dim), (shards_of,), jnp.float32, smallest / len(pieces), largest / len(pieces))
        loudness = loudness * jnp.repeat(jnp.exp(draws), dims[dim] // shards_of).reshape((-1,) + (1,) * (len(dims) - 1 - dim))
    return loudness


def bell_draw(own_key, dims, scale, bound, cuts=(), dtype=jnp.bfloat16):
    gain = level_of(own_key, dims, cuts, -0.22, 0.18) if cuts else 1.0
    values = jax.random.normal(own_key, dims, jnp.float32) * scale * gain
    return jnp.minimum(jnp.maximum(values, -bound), bound).astype(dtype)


def setup_inputs(seed: int = 0) -> dict:
    splits = jax.random.split(jax.random.key(seed), 4)
    return {
        "activations": bell_draw(splits[0], (TOKENS, D), 1.0, 6.0, ((0, 4), (1, 8)), jnp.float32),
        "weight_block": bell_draw(splits[1], (D, FF), D ** -0.5, 0.09375, ((0, 4), (1, 2)), jnp.float32),
        "cotangent": bell_draw(splits[2], (TOKENS, FF), 1.0, 6.0, ((0, 16), (1, 2)), jnp.float32),
    }


def silu_slope(preact):
    sig = jax.nn.sigmoid(preact)
    return sig * (1.0 + preact * (1.0 - sig))


def reference(activations, weight_block, cotangent):
    high = lax.Precision.HIGHEST
    preact = jnp.dot(activations, weight_block, precision=high, preferred_element_type=jnp.float32)
    output_act = jax.nn.silu(preact)
    pre_grad = cotangent * silu_slope(preact)
    input_grad = jnp.dot(pre_grad, weight_block.T, precision=high, preferred_element_type=jnp.float32)
    weight_grad = jnp.dot(activations.T, pre_grad, precision=high, preferred_element_type=jnp.float32)
    return output_act, input_grad, weight_grad
```

```python
import jax
import jax.numpy as jnp
from jax import lax
from jax.experimental import pallas as pl
from jax.experimental.pallas import tpu as pltpu
from jax.sharding import PartitionSpec as P

HIGH = lax.Precision.HIGH
CHUNKS = 6


def mm(lhs, rhs, contract):
    return lax.dot_general(
        lhs, rhs, (contract, ((), ())), precision=HIGH, preferred_element_type=jnp.float32
    )


def widths_of(total, parts):
    unit = 256 if total % 256 == 0 else total // 15
    count = total // unit
    base, extra = divmod(count, parts)
    return [(base + (1 if i < extra else 0)) * unit for i in range(parts)]


def unrotate(blocks, z, n):
    rev = jnp.concatenate([blocks[:1], blocks[1:][::-1]], 0)
    twice = jnp.concatenate([rev, rev], 0)
    return lax.dynamic_slice_in_dim(twice, lax.rem(n - z, n), n, 0)


def tie(value, *others):
    return lax.optimization_barrier((value,) + others)


def place(out, pieces, off, shape):
    half_d, h = pieces[0].shape

    def kernel(*refs):
        src, dst, (held, sem_in, sem_out) = refs[:4], refs[-4], refs[-3:]
        dp = lax.axis_index("dp")
        x, core = dp // 2, dp % 2
        loads, stores = [], []
        for i, (r, c) in enumerate(((core, x), (1 - core, x), (core, 1 - x), (1 - core, 1 - x))):
            rows = pl.ds(pl.multiple_of(r * half_d, 8), half_d)
            cols = pl.ds(pl.multiple_of(off + c * h, 128), h)
            loads.append(pltpu.make_async_copy(src[i], held.at[i], sem_in.at[i]))
            stores.append(pltpu.make_async_copy(held.at[i], dst.at[rows, cols], sem_out.at[i]))
        for load in loads:
            load.start()
        for load, store in zip(loads, stores):
            load.wait()
            store.start()
        for store in stores:
            store.wait()

    args = list(pieces) + ([] if out is None else [out])
    return pl.pallas_call(
        kernel,
        out_shape=jax.ShapeDtypeStruct(shape, jnp.float32),
        in_specs=[pl.BlockSpec(memory_space=pl.ANY)] * len(args),
        out_specs=pl.BlockSpec(memory_space=pl.ANY),
        scratch_shapes=[
            pltpu.VMEM((4, half_d, h), jnp.float32),
            pltpu.SemaphoreType.DMA((4,)),
            pltpu.SemaphoreType.DMA((4,)),
        ],
        compiler_params=pltpu.CompilerParams(vmem_limit_bytes=24 * 2**20),
        input_output_aliases={} if out is None else {4: 0},
        cost_estimate=pl.CostEstimate(flops=0, bytes_accessed=32 * half_d * h, transcendentals=0),
    )(*args)


def make_body(n, ncol):
    swap_x = [(0, 2), (2, 0), (1, 3), (3, 1)]
    swap_core = [(0, 1), (1, 0), (2, 3), (3, 2)]
    swap_y = [(0, 1), (1, 0)]

    def body(act, weight, cot):
        z = lax.axis_index("row")
        dp = lax.axis_index("dp")
        x, core = dp // 2, dp % 2
        y = lax.axis_index("col")
        tokens = act.shape[0]
        tb = tokens // n
        depth = weight.shape[0]
        ff = weight.shape[1]
        half_d = depth // 2

        def gather_y(v):
            if ncol != 2:
                return lax.all_gather(v, "col", axis=1, tiled=True)
            o = lax.ppermute(v, "col", swap_y)
            return jnp.where(y == 0, jnp.concatenate([v, o], 1), jnp.concatenate([o, v], 1))

        own = gather_y(act)
        other = gather_y(lax.ppermute(act, "dp", swap_x))
        both = jnp.stack([own.reshape(n, tb, depth), other.reshape(n, tb, depth)], 1)
        both = jnp.swapaxes(unrotate(both, z, n), 0, 1).reshape(2 * tokens, depth)

        widths = widths_of(ff, CHUNKS)
        offs = [sum(widths[:i]) for i in range(len(widths))]
        up_all = [(i, i + 1) for i in range(n - 1)]

        def up(v, lo, hi):
            return lax.ppermute(v, "row", up_all[lo:hi])

        def down(v, lo, hi):
            return lax.ppermute(v, "row", [(n - 1 - i, n - 1 - j) for i, j in up_all[lo:hi]])

        count = len(widths)
        part, acts, wg, got, ig_terms = {}, {}, {}, {}, []
        out = {}

        def forward(k):
            def run(lhs):
                off, wk = offs[k], widths[k]
                part[k] = mm(lhs, weight[:, off : off + wk], ((1,), (0,))).reshape(n, tb, wk)
                return [part[k]]

            return (lambda: [own]), run

        def weight_product(k):
            def ins():
                ups, dns = got[k]["ups"], got[k]["dns"]
                return [got[k]["g"]] + ups + dns

            def run(g, *recv):
                h = widths[k] // 2
                ups, dns = recv[: n - 1], recv[n - 1 :]
                blocks = [g] + [jnp.where(z > t, ups[t], dns[n - 2 - t]) for t in range(n - 1)]
                gz = jnp.concatenate([v[:, :h] for v in blocks] + [v[:, h:] for v in blocks], 0)
                full = mm(both, gz, ((0,), (0,)))
                keep = lax.dynamic_slice_in_dim(full, core * half_d, half_d, 0)
                give = lax.dynamic_slice_in_dim(full, (1 - core) * half_d, half_d, 0)
                wg[k] = {"gz": gz, "keep": keep, "in": lax.ppermute(give, "dp", swap_core)}
                return [keep]

            return ins, run

        def weight_sum(k):
            def run(keep, recv):
                keep = keep + recv
                wg[k]["keep"] = keep
                if k >= count - 2:
                    wg[k]["x"] = lax.ppermute(keep, "dp", swap_x)
                wg[k]["c"] = lax.ppermute(keep, "dp", swap_core)
                return [keep]

            return (lambda: [wg[k]["keep"], wg[k]["in"]]), run

        def weight_cross(k):
            def run(keep):
                wg[k]["x"] = lax.ppermute(keep, "dp", swap_x)
                return []

            return (lambda: [wg[k]["keep"]]), run

        def weight_back(k):
            def run(v):
                wg[k]["x"] = v
                wg[k]["xc"] = lax.ppermute(v, "dp", swap_core)
                return []

            return (lambda: [wg[k]["x"]]), run

        def weight_place(k):
            def run(*pieces):
                if ff % 256 == 0:
                    out["wg"] = place(out.get("wg"), pieces, offs[k], (depth, ff))
                    return []
                if "wg" not in out:
                    out["wg"] = jnp.zeros((depth, ff), jnp.float32)
                for i, piece in enumerate(pieces):
                    r, c = (core if i in (0, 2) else 1 - core), (x if i < 2 else 1 - x)
                    at = (r * half_d, offs[k] + c * (widths[k] // 2))
                    out["wg"] = lax.dynamic_update_slice(out["wg"], piece, at)
                return []

            return (lambda: [wg[k][i] for i in ("keep", "c", "x", "xc")]), run

        def input_product(k):
            def run(gz):
                h = widths[k] // 2
                wt = lax.dynamic_slice_in_dim(weight, offs[k] + x * h, h, 1)
                term = mm(gz, wt, ((1,), (1,)))
                out["ig"] = term if "ig" not in out else out["ig"] + term
                return [out["ig"]]

            return (lambda: [wg[k]["gz"]]), run

        events = {}
        for k in range(count):
            s, j = k % 2, k // 2
            first = 2 * j * n + s
            end = first + 4 * n - 4
            plan = [(first - 1, forward(k)), (end, weight_product(k)), (end + 1, weight_sum(k))]
            last = k >= count - 2
            cross = end + 1 if last else end + 4 + s
            plan += [] if last else [(cross, weight_cross(k))]
            plan += [(end + (2 if last else 5), input_product(k))]
            plan += [(cross + (1 if last else 3), weight_back(k)), (cross + (2 if last else 4), weight_place(k))]
            for when, what in plan:
                events.setdefault(when, []).append(what)

        done = []

        def half_slot(h, recv):
            nonlocal done
            todo = events.pop(h, [])
            ins = [what[0]() for what in todo]
            flat = tuple(v for group in ins for v in group)
            tied = lax.optimization_barrier(tuple(recv) + tuple(done) + flat)
            new = list(tied[: len(recv)])
            flat = list(tied[len(recv) + len(done) :])
            return new, todo, ins, flat

        def work(todo, ins, flat):
            nonlocal done
            done = []
            for what, group in zip(todo, ins):
                take, flat = flat[: len(group)], flat[len(group) :]
                done += what[1](*take)

        _, todo, ins, flat = half_slot(-1, [])
        work(todo, ins, flat)
        streams = [list(range(s, count, 2)) for s in (0, 1)]
        state = [{"rs": [], "ag": []}, {"rs": [], "ag": []}]
        steps = max(len(v) for v in streams) * n + n - 2
        for h in range(2 * steps):
            s, p = h % 2, h // 2
            st, j, t = state[s], p // n, p % n
            cur = streams[s][j] if j < len(streams[s]) else None
            prev = streams[s][j - 1] if 1 <= j <= len(streams[s]) else None
            same = len(st["rs"]) == 2 and len(st["ag"]) == 2 and st["rs"][0] is st["ag"][0]
            recv = list(st["ag"]) + ([] if same else list(st["rs"]))
            agg = None
            if st["ag"] and prev is not None:
                agg = prev if t < n - 1 else None
            new, todo, ins, flat = [], [], [], []
            if agg is not None:
                got[agg]["ups"].append(st["ag"][0])
                got[agg]["dns"].append(st["ag"][1])
            new, todo, ins, flat = half_slot(h, recv)
            ag = new[:2] if st["ag"] else []
            rs = (ag if same else new[len(ag) :]) if st["rs"] else []
            st["rs"], st["ag"] = [], []
            if t < n - 1:
                has_rs = cur is not None
                has_ag = prev is not None and t < n - 2
                if has_rs:
                    blk_u = lax.dynamic_index_in_dim(part[cur], jnp.clip(z + n - 1 - t, 0, n - 1), 0, keepdims=False)
                    blk_d = lax.dynamic_index_in_dim(part[cur], jnp.clip(z - n + 1 + t, 0, n - 1), 0, keepdims=False)
                merged = has_rs and has_ag and widths[cur] == widths[prev]
                if merged:
                    base = ag if t == 0 else rs
                    su = base[0] + jnp.where(z <= t, blk_u, 0.0)
                    sd = base[1] + jnp.where(n - 1 - z <= t, blk_d, 0.0)
                    st["rs"] = st["ag"] = [up(su, 0, n - 1), down(sd, 0, n - 1)]
                else:
                    if has_rs:
                        su, sd = (blk_u, blk_d) if t == 0 else (rs[0] + blk_u, rs[1] + blk_d)
                        st["rs"] = [up(su, 0, t + 1), down(sd, 0, t + 1)]
                    if has_ag:
                        st["ag"] = [up(ag[0], t + 1, n - 1), down(ag[1], t + 1, n - 1)]
            elif cur is not None:
                pre = lax.dynamic_index_in_dim(part[cur], z, 0, keepdims=False) + rs[0] + rs[1]
                off, wk = offs[cur], widths[cur]
                hw = wk // 2
                sig = jax.nn.sigmoid(pre)
                acts[cur] = pre * sig
                grad = cot[:, off : off + wk] * (sig * (1.0 + pre * (1.0 - sig)))
                left, right = grad[:, :hw], grad[:, hw:]
                mine = jnp.where(x == 0, left, right)
                theirs = jnp.where(x == 0, right, left)
                g = jnp.concatenate([mine, lax.ppermute(theirs, "dp", swap_x)], 1)
                got[cur] = {"g": g, "ups": [], "dns": []}
                st["ag"] = [up(g, 0, n - 1), down(g, 0, n - 1)]
            work(todo, ins, flat)
        for s in (0, 1):
            if state[s]["ag"]:
                got[streams[s][-1]]["ups"].append(state[s]["ag"][0])
                got[streams[s][-1]]["dns"].append(state[s]["ag"][1])
        for h in sorted(events):
            _, todo, ins, flat = half_slot(h, [])
            work(todo, ins, flat)
        ig, wg_out = out["ig"], out["wg"]
        acts = [acts[k] for k in range(count)]

        ig = ig.reshape(2, n, tb, depth)
        mine = ig[0] + lax.ppermute(ig[1], "dp", swap_x)
        if ncol != 2:
            mine = lax.psum_scatter(mine, "col", scatter_dimension=2, tiled=True)
        else:
            keep = lax.dynamic_slice_in_dim(mine, y * half_d, half_d, 2)
            give = lax.dynamic_slice_in_dim(mine, (1 - y) * half_d, half_d, 2)
            mine = keep + lax.ppermute(give, "col", swap_y)
        input_grad = unrotate(mine, z, n).reshape(tokens, -1)
        return jnp.concatenate(acts, 1), input_grad, wg_out

    return body


def solution(mesh):
    in_specs = (P("dp", ("row", "col")), P("row", "col"), P(("dp", "row"), "col"))
    out_specs = (P(("dp", "row"), "col"), P("dp", ("row", "col")), P("row", "col"))
    body = make_body(mesh.shape["row"], mesh.shape["col"])
    return jax.shard_map(body, mesh=mesh, in_specs=in_specs, out_specs=out_specs, check_vma=False)
```

```python
import jax
import jax.numpy as jnp
from jax import lax
from jax.experimental import pallas as pl
from jax.experimental.pallas import tpu as pltpu
from jax.sharding import PartitionSpec as P

HIGH = lax.Precision.HIGH
CHUNKS = 8


def mm(lhs, rhs, contract):
    return lax.dot_general(
        lhs, rhs, (contract, ((), ())), precision=HIGH, preferred_element_type=jnp.float32
    )


def widths_of(total, parts):
    unit = 2 * TILE if total % (2 * TILE) == 0 else total // 15
    count = total // unit
    base, extra = divmod(count, parts)
    return [(base + (1 if i < extra else 0)) * unit for i in range(parts)]


def unrotate(blocks, z, n):
    rev = jnp.concatenate([blocks[:1], blocks[1:][::-1]], 0)
    twice = jnp.concatenate([rev, rev], 0)
    return lax.dynamic_slice_in_dim(twice, lax.rem(n - z, n), n, 0)


def tie(value, *others):
    return lax.optimization_barrier((value,) + others)


def place(out, pieces, off, shape):
    half_d, h = pieces[0].shape

    def kernel(*refs):
        src, (dst, token, held, sem_in, sem_out) = refs[:4], refs[-5:]
        dp = lax.axis_index("dp")
        x, core = dp // 2, dp % 2
        loads, stores = [], []
        for i, (r, c) in enumerate(((core, x), (1 - core, x), (core, 1 - x), (1 - core, 1 - x))):
            rows = pl.ds(pl.multiple_of(r * half_d, 8), half_d)
            cols = pl.ds(pl.multiple_of(off + c * h, 128), h)
            loads.append(pltpu.make_async_copy(src[i], held.at[i], sem_in.at[i]))
            stores.append(pltpu.make_async_copy(held.at[i], dst.at[rows, cols], sem_out.at[i]))
        for load in loads:
            load.start()
        for load, store in zip(loads, stores):
            load.wait()
            store.start()
        for store in stores:
            store.wait()
        token[...] = jnp.zeros_like(token)

    args = list(pieces) + ([] if out is None else [out])
    return pl.pallas_call(
        kernel,
        out_shape=[
            jax.ShapeDtypeStruct(shape, jnp.float32),
            jax.ShapeDtypeStruct((8, 128), jnp.float32),
        ],
        in_specs=[pl.BlockSpec(memory_space=pl.ANY)] * len(args),
        out_specs=[pl.BlockSpec(memory_space=pl.ANY), pl.BlockSpec(memory_space=pltpu.VMEM)],
        scratch_shapes=[
            pltpu.VMEM((4, half_d, h), jnp.float32),
            pltpu.SemaphoreType.DMA((4,)),
            pltpu.SemaphoreType.DMA((4,)),
        ],
        compiler_params=pltpu.CompilerParams(vmem_limit_bytes=24 * 2**20),
        input_output_aliases={} if out is None else {4: 0},
        cost_estimate=LIGHT,
    )(*args)


TILE = 256
LIGHT = pl.CostEstimate(flops=1000, bytes_accessed=1000, transcendentals=0)


def cost_of(products):
    return pl.CostEstimate(flops=4 * products, bytes_accessed=1000, transcendentals=0)


def two(v):
    hi = v.astype(jnp.bfloat16)
    return hi, (v - hi.astype(jnp.float32)).astype(jnp.bfloat16)


def left3(v):
    hi = lax.reduce_precision(v, 8, 7)
    lo = (v - hi).astype(jnp.bfloat16)
    hi = hi.astype(jnp.bfloat16)
    return jnp.concatenate([hi, hi, lo], 1)


def forward_kernel(lhs3, weight, off, wk):
    rows, depth3 = lhs3.shape
    depth = depth3 // 3
    first = off // TILE

    def kernel(lhs_ref, w_ref, out_ref, w3):
        hi, lo = two(w_ref[...])
        w3[pl.ds(0, depth), :] = hi
        w3[pl.ds(depth, depth), :] = lo
        w3[pl.ds(2 * depth, depth), :] = hi

        out_ref[...] = jnp.dot(lhs_ref[...], w3[...], preferred_element_type=jnp.float32)

    return pl.pallas_call(
        kernel,
        grid=(wk // TILE,),
        in_specs=[
            pl.BlockSpec((rows, depth3), lambda j: (0, 0), pipeline_mode=pl.Buffered(1)),
            pl.BlockSpec((depth, TILE), lambda j: (0, first + j)),
        ],
        out_specs=pl.BlockSpec((rows, TILE), lambda j: (0, j)),
        out_shape=jax.ShapeDtypeStruct((rows, wk), jnp.float32),
        scratch_shapes=[pltpu.VMEM((depth3, TILE), jnp.bfloat16)],
        compiler_params=pltpu.CompilerParams(vmem_limit_bytes=40 * 2**20),
        cost_estimate=cost_of(rows * depth3 * wk),
    )(lhs3, weight)


def pick(own, oth, where, n, store):
    z = where[1]
    even = lax.rem(z, 2) == 0
    for side, group in enumerate((own, oth)):
        for q in range(n):
            if q == 0:
                v = group[0][...]
            else:
                below = jnp.where(even, group[n - 1 + q][...], group[q][...])
                above = jnp.where(even, group[n - q][...], group[2 * n - 1 - q][...])
                v = jnp.where(z >= q, below, above)
            store(side * n + q, *two(v))


def weight_kernel(place_of, at3, blocks, n):
    tb, wk = blocks[0].shape
    h = wk // 2
    tiles = h // TILE
    depth, toks3 = at3.shape
    toks = toks3 // 3
    half_d = depth // 2
    nb = len(blocks)

    def kernel(where, at_ref, *refs):
        keep_ref, give_ref, deep = refs[-3:]

        def store(q, hi, lo):
            for i, v in enumerate((hi, lo, hi)):
                deep[pl.ds(i * toks + q * tb, tb), :] = v

        pick(refs[:nb], refs[nb : 2 * nb], where, n, store)
        full = jnp.dot(at_ref[...], deep[...], preferred_element_type=jnp.float32)
        keep_ref[...] = full[:half_d]
        give_ref[...] = full[half_d:]

    return pl.pallas_call(
        kernel,
        grid_spec=pltpu.PrefetchScalarGridSpec(
            num_scalar_prefetch=1,
            grid=(tiles,),
            in_specs=[pl.BlockSpec((depth, toks3), lambda j, s: (0, 0), pipeline_mode=pl.Buffered(1))]
            + [pl.BlockSpec((tb, TILE), lambda j, s: (0, j))] * nb
            + [pl.BlockSpec((tb, TILE), lambda j, s: (0, tiles + j))] * nb,
            out_specs=[pl.BlockSpec((half_d, TILE), lambda j, s: (0, j))] * 2,
            scratch_shapes=[pltpu.VMEM((toks3, TILE), jnp.bfloat16)],
        ),
        out_shape=[jax.ShapeDtypeStruct((half_d, h), jnp.float32)] * 2,
        compiler_params=pltpu.CompilerParams(vmem_limit_bytes=40 * 2**20),
        cost_estimate=cost_of(depth * toks3 * h),
    )(place_of, at3, *blocks, *blocks)


def input_kernel(place_of, blocks, weight, acc, off, n):
    tb, wk = blocks[0].shape
    h = wk // 2
    tiles = h // TILE
    first = off // TILE
    depth = weight.shape[0]
    toks = 2 * n * tb
    nb = len(blocks)
    fresh = acc is None

    def kernel(where, w_ref, *refs):
        sum_ref, g_side, w_side = refs[-3:]

        def store(q, hi, lo):
            for i, v in enumerate((hi, hi, lo)):
                g_side[pl.ds(q * tb, tb), pl.ds(i * TILE, TILE)] = v

        pick(refs[:nb], refs[nb : 2 * nb], where, n, store)
        hi, lo = two(w_ref[...])
        for i, v in enumerate((hi, lo, hi)):
            w_side[:, pl.ds(i * TILE, TILE)] = v
        term = lax.dot_general(
            g_side[...], w_side[...], (((1,), (1,)), ((), ())), preferred_element_type=jnp.float32
        )

        @pl.when(pl.program_id(0) == 0)
        def _():
            sum_ref[...] = term if fresh else refs[2 * nb][...] + term

        @pl.when(pl.program_id(0) > 0)
        def _():
            sum_ref[...] = sum_ref[...] + term

    whole = pl.BlockSpec((toks, depth), lambda j, s: (0, 0), pipeline_mode=pl.Buffered(1))
    args = [place_of, weight, *blocks, *blocks] + ([] if fresh else [acc])
    return pl.pallas_call(
        kernel,
        grid_spec=pltpu.PrefetchScalarGridSpec(
            num_scalar_prefetch=1,
            grid=(tiles,),
            in_specs=[pl.BlockSpec((depth, TILE), lambda j, s: (0, first + s[0] * tiles + j))]
            + [pl.BlockSpec((tb, TILE), lambda j, s: (0, j))] * nb
            + [pl.BlockSpec((tb, TILE), lambda j, s: (0, tiles + j))] * nb
            + ([] if fresh else [whole]),
            out_specs=whole,
            scratch_shapes=[
                pltpu.VMEM((toks, 3 * TILE), jnp.bfloat16),
                pltpu.VMEM((depth, 3 * TILE), jnp.bfloat16),
            ],
        ),
        out_shape=jax.ShapeDtypeStruct((toks, depth), jnp.float32),
        input_output_aliases={} if fresh else {len(args) - 1: 0},
        compiler_params=pltpu.CompilerParams(vmem_limit_bytes=40 * 2**20),
        cost_estimate=cost_of(3 * toks * depth * h),
    )(*args)


def make_body(n, ncol):
    swap_x = [(0, 2), (2, 0), (1, 3), (3, 1)]
    swap_core = [(0, 1), (1, 0), (2, 3), (3, 2)]
    swap_y = [(0, 1), (1, 0)]

    def body(act, weight, cot):
        z = lax.axis_index("row")
        dp = lax.axis_index("dp")
        x, core = dp // 2, dp % 2
        y = lax.axis_index("col")
        tokens = act.shape[0]
        tb = tokens // n
        depth = weight.shape[0]
        ff = weight.shape[1]
        half_d = depth // 2

        def gather_y(v):
            if ncol != 2:
                return lax.all_gather(v, "col", axis=1, tiled=True)
            o = lax.ppermute(v, "col", swap_y)
            return jnp.where(y == 0, jnp.concatenate([v, o], 1), jnp.concatenate([o, v], 1))

        own = gather_y(act)
        other = gather_y(lax.ppermute(act, "dp", swap_x))
        both = jnp.stack([own.reshape(n, tb, depth), other.reshape(n, tb, depth)], 1)
        both = jnp.swapaxes(unrotate(both, z, n), 0, 1).reshape(2 * tokens, depth)

        widths = widths_of(ff, CHUNKS)
        offs = [sum(widths[:i]) for i in range(len(widths))]
        even = z % 2 == 0

        def exchange(su, sd, lo, hi):
            pairs = ([], [])
            for i in range(lo, hi):
                pairs[i % 2].append((i, i + 1))
                pairs[(n - 2 - i) % 2].append((n - 1 - i, n - 2 - i))
            first, second = (su, su) if su is sd else (jnp.where(even, su, sd), jnp.where(even, sd, su))
            return [
                lax.ppermute(v, "row", p) if p else jnp.zeros_like(v)
                for v, p in zip((first, second), pairs)
            ]

        def came(pair):
            return [jnp.where(even, pair[1], pair[0]), jnp.where(even, pair[0], pair[1])]

        halves = jnp.stack([both[:, :half_d], both[:, half_d:]])
        both = jnp.concatenate([halves[core], halves[1 - core]], 1)
        kernels = ff % (2 * TILE) == 0 and depth % (2 * TILE) == 0 and tokens % TILE == 0
        own_in = own
        if kernels:
            own_in, at3 = left3(own), left3(both.T)
            place_of = jnp.stack([x, z]).astype(jnp.int32)

        count = len(widths)
        part, acts, wg, got, ig_terms = {}, {}, {}, {}, []
        out = {}

        def forward(k):
            def run(lhs):
                off, wk = offs[k], widths[k]
                if kernels:
                    part[k] = forward_kernel(lhs, weight, off, wk).reshape(n, tb, wk)
                else:
                    part[k] = mm(lhs, weight[:, off : off + wk], ((1,), (0,))).reshape(n, tb, wk)
                return [part[k]]

            return (lambda: [own_in]), run

        def weight_product(k):
            def ins():
                ups, dns = got[k]["ups"], got[k]["dns"]
                return [got[k]["g"]] + ups + dns

            def run(g, *recv):
                h = widths[k] // 2
                if kernels:
                    keep, give = weight_kernel(place_of, at3, [g, *recv], n)
                    wg[k] = {"keep": keep, "in": lax.ppermute(give, "dp", swap_core)}
                    return [keep]
                pairs = [came(v) for v in zip(recv[: n - 1], recv[n - 1 :])]
                ups, dns = [v[0] for v in pairs], [v[1] for v in pairs]
                blocks = [g] + [jnp.where(z > t, ups[t], dns[n - 2 - t]) for t in range(n - 1)]
                gz = jnp.concatenate([v[:, :h] for v in blocks] + [v[:, h:] for v in blocks], 0)
                full = mm(both, gz, ((0,), (0,)))
                keep, give = full[:half_d], full[half_d:]
                wg[k] = {"gz": gz, "keep": keep, "in": lax.ppermute(give, "dp", swap_core)}
                return [keep]

            return ins, run

        def weight_sum(k):
            def run(keep, recv):
                keep = keep + recv
                wg[k]["keep"] = keep
                if k >= count - 2:
                    wg[k]["x"] = lax.ppermute(keep, "dp", swap_x)
                wg[k]["c"] = lax.ppermute(keep, "dp", swap_core)
                return [keep]

            return (lambda: [wg[k]["keep"], wg[k]["in"]]), run

        def weight_cross(k):
            def run(keep):
                wg[k]["x"] = lax.ppermute(keep, "dp", swap_x)
                return []

            return (lambda: [wg[k]["keep"]]), run

        def weight_back(k):
            def run(v):
                wg[k]["x"] = v
                wg[k]["xc"] = lax.ppermute(v, "dp", swap_core)
                return []

            return (lambda: [wg[k]["x"]]), run

        def weight_place(k):
            def run(*pieces):
                if ff % 256 == 0:
                    out["wg"], token = place(out.get("wg"), pieces, offs[k], (depth, ff))
                    return [token]
                if "wg" not in out:
                    out["wg"] = jnp.zeros((depth, ff), jnp.float32)
                for i, piece in enumerate(pieces):
                    r, c = (core if i in (0, 2) else 1 - core), (x if i < 2 else 1 - x)
                    at = (r * half_d, offs[k] + c * (widths[k] // 2))
                    out["wg"] = lax.dynamic_update_slice(out["wg"], piece, at)
                return []

            return (lambda: [wg[k][i] for i in ("keep", "c", "x", "xc")]), run

        def input_product(k):
            def run(gz):
                h = widths[k] // 2
                wt = lax.dynamic_slice_in_dim(weight, offs[k] + x * h, h, 1)
                term = mm(gz, wt, ((1,), (1,)))
                out["ig"] = term if "ig" not in out else out["ig"] + term
                return [out["ig"]]

            return (lambda: [wg[k]["gz"]]), run

        def input_blocks(k):
            def run(*blocks):
                out["ig"] = input_kernel(place_of, blocks, weight, out.get("ig"), offs[k], n)
                return [out["ig"]]

            return weight_product(k)[0], run

        events = {}
        for k in range(count):
            s, j = k % 2, k // 2
            first = 2 * j * n + s
            end = first + 4 * n - 4
            last = k >= count - 2
            plan = [(end if last else end + 5, input_blocks(k))] if kernels else []
            plan += [(first - (1 if k < 2 else 2), forward(k)), (end, weight_product(k))]
            plan += [(end + (1 if last else 2), weight_sum(k))]
            cross = end + 1 if last else end + 4 + s
            plan += [] if last else [(cross, weight_cross(k))]
            plan += [] if kernels else [(end + (2 if last else 5), input_product(k))]
            plan += [(cross + (1 if last else 2), weight_back(k)), (cross + (2 if last else 3), weight_place(k))]
            for when, what in plan:
                events.setdefault(when, []).append(what)

        done, before = [], []

        def half_slot(h, recv):
            todo = events.pop(h, [])
            ins = [what[0]() for what in todo]
            flat = tuple(v for group in ins for v in group)
            tied = lax.optimization_barrier(tuple(recv) + tuple(before) + flat)
            new = list(tied[: len(recv)])
            flat = list(tied[len(recv) + len(before) :])
            return new, todo, ins, flat

        def work(todo, ins, flat):
            nonlocal done, before
            done, before = [], done
            for what, group in zip(todo, ins):
                take, flat = flat[: len(group)], flat[len(group) :]
                done += what[1](*take)

        _, todo, ins, flat = half_slot(-1, [])
        work(todo, ins, flat)
        streams = [list(range(s, count, 2)) for s in (0, 1)]
        state = [{"rs": [], "ag": []}, {"rs": [], "ag": []}]
        steps = max(len(v) for v in streams) * n + n - 2
        for h in range(2 * steps):
            s, p = h % 2, h // 2
            st, j, t = state[s], p // n, p % n
            cur = streams[s][j] if j < len(streams[s]) else None
            prev = streams[s][j - 1] if 1 <= j <= len(streams[s]) else None
            same = len(st["rs"]) == 2 and len(st["ag"]) == 2 and st["rs"][0] is st["ag"][0]
            recv = list(st["ag"]) + ([] if same else list(st["rs"]))
            agg = None
            if st["ag"] and prev is not None:
                agg = prev if t < n - 1 else None
            new, todo, ins, flat = [], [], [], []
            if agg is not None:
                got[agg]["ups"].append(st["ag"][0])
                got[agg]["dns"].append(st["ag"][1])
            new, todo, ins, flat = half_slot(h, recv)
            ag = new[:2] if st["ag"] else []
            rs = (ag if same else new[len(ag) :]) if st["rs"] else []
            ag, rs = (came(v) if v else [] for v in (ag, rs))
            st["rs"], st["ag"] = [], []
            if t < n - 1:
                has_rs = cur is not None
                has_ag = prev is not None and t < n - 2
                if has_rs:
                    blk_u = lax.dynamic_index_in_dim(part[cur], jnp.clip(z + n - 1 - t, 0, n - 1), 0, keepdims=False)
                    blk_d = lax.dynamic_index_in_dim(part[cur], jnp.clip(z - n + 1 + t, 0, n - 1), 0, keepdims=False)
                merged = has_rs and has_ag and widths[cur] == widths[prev]
                if merged:
                    base = ag if t == 0 else rs
                    su = base[0] + jnp.where(z <= t, blk_u, 0.0)
                    sd = base[1] + jnp.where(n - 1 - z <= t, blk_d, 0.0)
                    st["rs"] = st["ag"] = exchange(su, sd, 0, n - 1)
                else:
                    if has_rs:
                        su, sd = (blk_u, blk_d) if t == 0 else (rs[0] + blk_u, rs[1] + blk_d)
                        st["rs"] = exchange(su, sd, 0, t + 1)
                    if has_ag:
                        st["ag"] = exchange(ag[0], ag[1], t + 1, n - 1)
            elif cur is not None:
                pre = lax.dynamic_index_in_dim(part[cur], z, 0, keepdims=False) + rs[0] + rs[1]
                off, wk = offs[cur], widths[cur]
                hw = wk // 2
                sig = jax.nn.sigmoid(pre)
                acts[cur] = pre * sig
                grad = cot[:, off : off + wk] * (sig * (1.0 + pre * (1.0 - sig)))
                left, right = grad[:, :hw], grad[:, hw:]
                mine = jnp.where(x == 0, left, right)
                theirs = jnp.where(x == 0, right, left)
                g = jnp.concatenate([mine, lax.ppermute(theirs, "dp", swap_x)], 1)
                got[cur] = {"g": g, "ups": [], "dns": []}
                st["ag"] = exchange(g, g, 0, n - 1)
            work(todo, ins, flat)
        for s in (0, 1):
            if state[s]["ag"]:
                got[streams[s][-1]]["ups"].append(state[s]["ag"][0])
                got[streams[s][-1]]["dns"].append(state[s]["ag"][1])
        for h in sorted(events):
            _, todo, ins, flat = half_slot(h, [])
            work(todo, ins, flat)
        ig, wg_out = out["ig"], out["wg"]
        acts = [acts[k] for k in range(count)]

        ig = ig.reshape(2, n, tb, depth)
        def over_x(v):
            return v[0] + lax.ppermute(v[1], "dp", swap_x)

        def over_y(v):
            if ncol != 2:
                return lax.psum_scatter(v, "col", scatter_dimension=v.ndim - 1, tiled=True)
            left, right = v[..., :half_d], v[..., half_d:]
            keep, give = jnp.where(y == 0, left, right), jnp.where(y == 0, right, left)
            return keep + lax.ppermute(give, "col", swap_y)

        mid = n // 2
        mine = jnp.concatenate([over_y(over_x(ig[:, :mid])), over_x(over_y(ig[:, mid:]))], 0)
        input_grad = unrotate(mine, z, n).reshape(tokens, -1)
        return jnp.concatenate(acts, 1), input_grad, wg_out

    return body


def solution(mesh):
    in_specs = (P("dp", ("row", "col")), P("row", "col"), P(("dp", "row"), "col"))
    out_specs = (P(("dp", "row"), "col"), P("dp", ("row", "col")), P("row", "col"))
    body = make_body(mesh.shape["row"], mesh.shape["col"])
    return jax.shard_map(body, mesh=mesh, in_specs=in_specs, out_specs=out_specs, check_vma=False)
```

```python
import jax
import jax.numpy as jnp
from jax import lax
from jax.experimental import pallas as pl
from jax.experimental.pallas import tpu as pltpu
from jax.sharding import PartitionSpec as P

HIGH = lax.Precision.HIGH
CHUNKS = 8


def mm(lhs, rhs, contract):
    return lax.dot_general(
        lhs, rhs, (contract, ((), ())), precision=HIGH, preferred_element_type=jnp.float32
    )


def widths_of(total, parts):
    unit = 2 * TILE if total % (2 * TILE) == 0 else total // 15
    count = total // unit
    base, extra = divmod(count, parts)
    return [(base + (1 if i < extra else 0)) * unit for i in range(parts)]


def unrotate(blocks, z, n):
    rev = jnp.concatenate([blocks[:1], blocks[1:][::-1]], 0)
    twice = jnp.concatenate([rev, rev], 0)
    return lax.dynamic_slice_in_dim(twice, lax.rem(n - z, n), n, 0)


def tie(value, *others):
    return lax.optimization_barrier((value,) + others)


def place(out, after, pieces, off, shape):
    half_d, h = pieces[0].shape

    def kernel(*refs):
        src, (dst, token, held, sem_in, sem_out) = refs[:4], refs[-5:]
        dp = lax.axis_index("dp")
        x, core = dp // 2, dp % 2
        loads, stores = [], []
        for i, (r, c) in enumerate(((core, x), (1 - core, x), (core, 1 - x), (1 - core, 1 - x))):
            rows = pl.ds(pl.multiple_of(r * half_d, 8), half_d)
            cols = pl.ds(pl.multiple_of(off + c * h, 128), h)
            loads.append(pltpu.make_async_copy(src[i], held.at[i], sem_in.at[i]))
            stores.append(pltpu.make_async_copy(held.at[i], dst.at[rows, cols], sem_out.at[i]))
        for load in loads:
            load.start()
        for load, store in zip(loads, stores):
            load.wait()
            store.start()
        for store in stores:
            store.wait()
        token[...] = jnp.zeros_like(token)

    args = list(pieces) + ([] if out is None else [out, after])
    return pl.pallas_call(
        kernel,
        out_shape=[
            jax.ShapeDtypeStruct(shape, jnp.float32),
            jax.ShapeDtypeStruct((8, 128), jnp.float32),
        ],
        in_specs=[pl.BlockSpec(memory_space=pl.ANY)] * len(args),
        out_specs=[pl.BlockSpec(memory_space=pl.ANY), pl.BlockSpec(memory_space=pltpu.VMEM)],
        scratch_shapes=[
            pltpu.VMEM((4, half_d, h), jnp.float32),
            pltpu.SemaphoreType.DMA((4,)),
            pltpu.SemaphoreType.DMA((4,)),
        ],
        compiler_params=pltpu.CompilerParams(vmem_limit_bytes=24 * 2**20),
        input_output_aliases={} if out is None else {4: 0},
        cost_estimate=LIGHT,
    )(*args)


TILE = 256
LIGHT = pl.CostEstimate(flops=1000, bytes_accessed=1000, transcendentals=0)


def cost_of(products):
    return pl.CostEstimate(flops=4 * products, bytes_accessed=1000, transcendentals=0)


def two(v):
    hi = v.astype(jnp.bfloat16)
    return hi, (v - hi.astype(jnp.float32)).astype(jnp.bfloat16)


def left3(v):
    hi = lax.reduce_precision(v, 8, 7)
    lo = (v - hi).astype(jnp.bfloat16)
    hi = hi.astype(jnp.bfloat16)
    return jnp.concatenate([hi, hi, lo], 1)


def forward_kernel(lhs3, weight, off, wk):
    rows, depth3 = lhs3.shape
    depth = depth3 // 3
    first = off // TILE

    def kernel(lhs_ref, w_ref, out_ref, w3):
        hi, lo = two(w_ref[...])
        w3[pl.ds(0, depth), :] = hi
        w3[pl.ds(depth, depth), :] = lo
        w3[pl.ds(2 * depth, depth), :] = hi

        out_ref[...] = jnp.dot(lhs_ref[...], w3[...], preferred_element_type=jnp.float32)

    return pl.pallas_call(
        kernel,
        grid=(wk // TILE,),
        in_specs=[
            pl.BlockSpec((rows, depth3), lambda j: (0, 0), pipeline_mode=pl.Buffered(1)),
            pl.BlockSpec((depth, TILE), lambda j: (0, first + j)),
        ],
        out_specs=pl.BlockSpec((rows, TILE), lambda j: (0, j)),
        out_shape=jax.ShapeDtypeStruct((rows, wk), jnp.float32),
        scratch_shapes=[pltpu.VMEM((depth3, TILE), jnp.bfloat16)],
        compiler_params=pltpu.CompilerParams(vmem_limit_bytes=40 * 2**20),
        cost_estimate=cost_of(rows * depth3 * wk),
    )(lhs3, weight)


def pick(own, oth, where, n, store):
    z = where[1]
    even = lax.rem(z, 2) == 0
    for side, group in enumerate((own, oth)):
        for q in range(n):
            if q == 0:
                v = group[0][...]
            else:
                below = jnp.where(even, group[n - 1 + q][...], group[q][...])
                above = jnp.where(even, group[n - q][...], group[2 * n - 1 - q][...])
                v = jnp.where(z >= q, below, above)
            store(side * n + q, *two(v))


def weight_kernel(place_of, at3, blocks, n):
    tb, wk = blocks[0].shape
    h = wk // 2
    tiles = h // TILE
    depth, toks3 = at3.shape
    toks = toks3 // 3
    half_d = depth // 2
    nb = len(blocks)

    def kernel(where, at_ref, *refs):
        keep_ref, give_ref, deep = refs[-3:]

        def store(q, hi, lo):
            for i, v in enumerate((hi, lo, hi)):
                deep[pl.ds(i * toks + q * tb, tb), :] = v

        pick(refs[:nb], refs[nb : 2 * nb], where, n, store)
        full = jnp.dot(at_ref[...], deep[...], preferred_element_type=jnp.float32)
        keep_ref[...] = full[:half_d]
        give_ref[...] = full[half_d:]

    return pl.pallas_call(
        kernel,
        grid_spec=pltpu.PrefetchScalarGridSpec(
            num_scalar_prefetch=1,
            grid=(tiles,),
            in_specs=[pl.BlockSpec((depth, toks3), lambda j, s: (0, 0), pipeline_mode=pl.Buffered(1))]
            + [pl.BlockSpec((tb, TILE), lambda j, s: (0, j))] * nb
            + [pl.BlockSpec((tb, TILE), lambda j, s: (0, tiles + j))] * nb,
            out_specs=[pl.BlockSpec((half_d, TILE), lambda j, s: (0, j))] * 2,
            scratch_shapes=[pltpu.VMEM((toks3, TILE), jnp.bfloat16)],
        ),
        out_shape=[jax.ShapeDtypeStruct((half_d, h), jnp.float32)] * 2,
        compiler_params=pltpu.CompilerParams(vmem_limit_bytes=40 * 2**20),
        cost_estimate=cost_of(depth * toks3 * h),
    )(place_of, at3, *blocks, *blocks)


def input_kernel(place_of, blocks, weight, acc, off, n):
    tb, wk = blocks[0].shape
    h = wk // 2
    tiles = h // TILE
    first = off // TILE
    depth = weight.shape[0]
    toks = 2 * n * tb
    nb = len(blocks)
    fresh = acc is None

    def kernel(where, w_ref, *refs):
        sum_ref, g_side, w_side = refs[-3:]

        def store(q, hi, lo):
            for i, v in enumerate((hi, hi, lo)):
                g_side[pl.ds(q * tb, tb), pl.ds(i * TILE, TILE)] = v

        pick(refs[:nb], refs[nb : 2 * nb], where, n, store)
        hi, lo = two(w_ref[...])
        for i, v in enumerate((hi, lo, hi)):
            w_side[:, pl.ds(i * TILE, TILE)] = v
        term = lax.dot_general(
            g_side[...], w_side[...], (((1,), (1,)), ((), ())), preferred_element_type=jnp.float32
        )

        @pl.when(pl.program_id(0) == 0)
        def _():
            sum_ref[...] = term if fresh else refs[2 * nb][...] + term

        @pl.when(pl.program_id(0) > 0)
        def _():
            sum_ref[...] = sum_ref[...] + term

    whole = pl.BlockSpec((toks, depth), lambda j, s: (0, 0), pipeline_mode=pl.Buffered(1))
    args = [place_of, weight, *blocks, *blocks] + ([] if fresh else [acc])
    return pl.pallas_call(
        kernel,
        grid_spec=pltpu.PrefetchScalarGridSpec(
            num_scalar_prefetch=1,
            grid=(tiles,),
            in_specs=[pl.BlockSpec((depth, TILE), lambda j, s: (0, first + s[0] * tiles + j))]
            + [pl.BlockSpec((tb, TILE), lambda j, s: (0, j))] * nb
            + [pl.BlockSpec((tb, TILE), lambda j, s: (0, tiles + j))] * nb
            + ([] if fresh else [whole]),
            out_specs=whole,
            scratch_shapes=[
                pltpu.VMEM((toks, 3 * TILE), jnp.bfloat16),
                pltpu.VMEM((depth, 3 * TILE), jnp.bfloat16),
            ],
        ),
        out_shape=jax.ShapeDtypeStruct((toks, depth), jnp.float32),
        input_output_aliases={} if fresh else {len(args) - 1: 0},
        compiler_params=pltpu.CompilerParams(vmem_limit_bytes=40 * 2**20),
        cost_estimate=cost_of(3 * toks * depth * h),
    )(*args)


def make_body(n, ncol):
    swap_x = [(0, 2), (2, 0), (1, 3), (3, 1)]
    swap_core = [(0, 1), (1, 0), (2, 3), (3, 2)]
    swap_y = [(0, 1), (1, 0)]

    def body(act, weight, cot):
        z = lax.axis_index("row")
        dp = lax.axis_index("dp")
        x, core = dp // 2, dp % 2
        y = lax.axis_index("col")
        tokens = act.shape[0]
        tb = tokens // n
        depth = weight.shape[0]
        ff = weight.shape[1]
        half_d = depth // 2

        def gather_y(v):
            if ncol != 2:
                return lax.all_gather(v, "col", axis=1, tiled=True)
            o = lax.ppermute(v, "col", swap_y)
            return jnp.where(y == 0, jnp.concatenate([v, o], 1), jnp.concatenate([o, v], 1))

        own = gather_y(act)
        other = gather_y(lax.ppermute(act, "dp", swap_x))
        both = jnp.stack([own.reshape(n, tb, depth), other.reshape(n, tb, depth)], 1)
        both = jnp.swapaxes(unrotate(both, z, n), 0, 1).reshape(2 * tokens, depth)

        widths = widths_of(ff, CHUNKS)
        offs = [sum(widths[:i]) for i in range(len(widths))]
        even = z % 2 == 0

        def exchange(su, sd, lo, hi):
            pairs = ([], [])
            for i in range(lo, hi):
                pairs[i % 2].append((i, i + 1))
                pairs[(n - 2 - i) % 2].append((n - 1 - i, n - 2 - i))
            first, second = (su, su) if su is sd else (jnp.where(even, su, sd), jnp.where(even, sd, su))
            return [
                lax.ppermute(v, "row", p) if p else jnp.zeros_like(v)
                for v, p in zip((first, second), pairs)
            ]

        def came(pair):
            return [jnp.where(even, pair[1], pair[0]), jnp.where(even, pair[0], pair[1])]

        halves = jnp.stack([both[:, :half_d], both[:, half_d:]])
        both = jnp.concatenate([halves[core], halves[1 - core]], 1)
        kernels = ff % (2 * TILE) == 0 and depth % (2 * TILE) == 0 and tokens % TILE == 0
        own_in = own
        if kernels:
            own_in, at3 = left3(own), left3(both.T)
            place_of = jnp.stack([x, z]).astype(jnp.int32)

        count = len(widths)
        part, acts, wg, got, ig_terms = {}, {}, {}, {}, []
        out = {}

        def forward(k):
            def run(lhs):
                off, wk = offs[k], widths[k]
                if kernels:
                    part[k] = forward_kernel(lhs, weight, off, wk).reshape(n, tb, wk)
                else:
                    part[k] = mm(lhs, weight[:, off : off + wk], ((1,), (0,))).reshape(n, tb, wk)
                return [part[k]]

            return (lambda: [own_in]), run

        def weight_product(k):
            def ins():
                ups, dns = got[k]["ups"], got[k]["dns"]
                return [got[k]["g"]] + ups + dns

            def run(g, *recv):
                h = widths[k] // 2
                if kernels:
                    keep, give = weight_kernel(place_of, at3, [g, *recv], n)
                    wg[k] = {"keep": keep, "in": lax.ppermute(give, "dp", swap_core)}
                    return [keep]
                pairs = [came(v) for v in zip(recv[: n - 1], recv[n - 1 :])]
                ups, dns = [v[0] for v in pairs], [v[1] for v in pairs]
                blocks = [g] + [jnp.where(z > t, ups[t], dns[n - 2 - t]) for t in range(n - 1)]
                gz = jnp.concatenate([v[:, :h] for v in blocks] + [v[:, h:] for v in blocks], 0)
                full = mm(both, gz, ((0,), (0,)))
                keep, give = full[:half_d], full[half_d:]
                wg[k] = {"gz": gz, "keep": keep, "in": lax.ppermute(give, "dp", swap_core)}
                return [keep]

            return ins, run

        def weight_sum(k):
            def run(keep, recv):
                keep = keep + recv
                wg[k]["keep"] = keep
                if k >= count - 2:
                    wg[k]["x"] = lax.ppermute(keep, "dp", swap_x)
                wg[k]["c"] = lax.ppermute(keep, "dp", swap_core)
                return [keep]

            return (lambda: [wg[k]["keep"], wg[k]["in"]]), run

        def weight_cross(k):
            def run(keep):
                wg[k]["x"] = lax.ppermute(keep, "dp", swap_x)
                return []

            return (lambda: [wg[k]["keep"]]), run

        def weight_back(k):
            def run(v):
                wg[k]["x"] = v
                wg[k]["xc"] = lax.ppermute(v, "dp", swap_core)
                return []

            return (lambda: [wg[k]["x"]]), run

        def weight_place(k):
            def run(*pieces):
                if ff % 256 == 0:
                    out["wg"], out["after"] = place(
                        out.get("wg"), out.get("after"), pieces, offs[k], (depth, ff)
                    )
                    return [out["after"]]
                if "wg" not in out:
                    out["wg"] = jnp.zeros((depth, ff), jnp.float32)
                for i, piece in enumerate(pieces):
                    r, c = (core if i in (0, 2) else 1 - core), (x if i < 2 else 1 - x)
                    at = (r * half_d, offs[k] + c * (widths[k] // 2))
                    out["wg"] = lax.dynamic_update_slice(out["wg"], piece, at)
                return []

            return (lambda: [wg[k][i] for i in ("keep", "c", "x", "xc")]), run

        def input_product(k):
            def run(gz):
                h = widths[k] // 2
                wt = lax.dynamic_slice_in_dim(weight, offs[k] + x * h, h, 1)
                term = mm(gz, wt, ((1,), (1,)))
                out["ig"] = term if "ig" not in out else out["ig"] + term
                return [out["ig"]]

            return (lambda: [wg[k]["gz"]]), run

        def input_blocks(k):
            def run(*blocks):
                out["ig"] = input_kernel(place_of, blocks, weight, out.get("ig"), offs[k], n)
                return [out["ig"]]

            return weight_product(k)[0], run

        events = {}
        for k in range(count):
            s, j = k % 2, k // 2
            first = 2 * j * n + s
            end = first + 4 * n - 4
            last = k >= count - 2
            plan = [(end if last else end + 5, input_blocks(k))] if kernels else []
            plan += [(first - (1 if k < 2 else 2), forward(k)), (end, weight_product(k))]
            plan += [(end + (1 if last else 2), weight_sum(k))]
            cross = end + 1 if last else end + 4 + s
            plan += [] if last else [(cross, weight_cross(k))]
            plan += [] if kernels else [(end + (2 if last else 5), input_product(k))]
            when = cross + 2 if last else max(cross + 3, 2 * n * ((count + 1) // 2) - 2 + k)
            plan += [(cross + (1 if last else 2), weight_back(k)), (when, weight_place(k))]
            for when, what in plan:
                events.setdefault(when, []).append(what)

        done, before = [], []

        def half_slot(h, recv):
            todo = events.pop(h, [])
            ins = [what[0]() for what in todo]
            flat = tuple(v for group in ins for v in group)
            tied = lax.optimization_barrier(tuple(recv) + tuple(before) + flat)
            new = list(tied[: len(recv)])
            for was, now in zip(before, tied[len(recv) :]):
                if was is out.get("after"):
                    out["after"] = now
            flat = list(tied[len(recv) + len(before) :])
            return new, todo, ins, flat

        def work(todo, ins, flat):
            nonlocal done, before
            done, before = [], done
            for what, group in zip(todo, ins):
                take, flat = flat[: len(group)], flat[len(group) :]
                done += what[1](*take)

        _, todo, ins, flat = half_slot(-1, [])
        work(todo, ins, flat)
        streams = [list(range(s, count, 2)) for s in (0, 1)]
        state = [{"rs": [], "ag": []}, {"rs": [], "ag": []}]
        steps = max(len(v) for v in streams) * n + n - 2
        for h in range(2 * steps):
            s, p = h % 2, h // 2
            st, j, t = state[s], p // n, p % n
            cur = streams[s][j] if j < len(streams[s]) else None
            prev = streams[s][j - 1] if 1 <= j <= len(streams[s]) else None
            same = len(st["rs"]) == 2 and len(st["ag"]) == 2 and st["rs"][0] is st["ag"][0]
            recv = list(st["ag"]) + ([] if same else list(st["rs"]))
            agg = None
            if st["ag"] and prev is not None:
                agg = prev if t < n - 1 else None
            new, todo, ins, flat = [], [], [], []
            if agg is not None:
                got[agg]["ups"].append(st["ag"][0])
                got[agg]["dns"].append(st["ag"][1])
            new, todo, ins, flat = half_slot(h, recv)
            ag = new[:2] if st["ag"] else []
            rs = (ag if same else new[len(ag) :]) if st["rs"] else []
            ag, rs = (came(v) if v else [] for v in (ag, rs))
            st["rs"], st["ag"] = [], []
            if t < n - 1:
                has_rs = cur is not None
                has_ag = prev is not None and t < n - 2
                if has_rs:
                    blk_u = lax.dynamic_index_in_dim(part[cur], jnp.clip(z + n - 1 - t, 0, n - 1), 0, keepdims=False)
                    blk_d = lax.dynamic_index_in_dim(part[cur], jnp.clip(z - n + 1 + t, 0, n - 1), 0, keepdims=False)
                merged = has_rs and has_ag and widths[cur] == widths[prev]
                if merged:
                    base = ag if t == 0 else rs
                    su = base[0] + jnp.where(z <= t, blk_u, 0.0)
                    sd = base[1] + jnp.where(n - 1 - z <= t, blk_d, 0.0)
                    st["rs"] = st["ag"] = exchange(su, sd, 0, n - 1)
                else:
                    if has_rs:
                        su, sd = (blk_u, blk_d) if t == 0 else (rs[0] + blk_u, rs[1] + blk_d)
                        st["rs"] = exchange(su, sd, 0, t + 1)
                    if has_ag:
                        st["ag"] = exchange(ag[0], ag[1], t + 1, n - 1)
            elif cur is not None:
                pre = lax.dynamic_index_in_dim(part[cur], z, 0, keepdims=False) + rs[0] + rs[1]
                off, wk = offs[cur], widths[cur]
                hw = wk // 2
                sig = jax.nn.sigmoid(pre)
                acts[cur] = pre * sig
                grad = cot[:, off : off + wk] * (sig * (1.0 + pre * (1.0 - sig)))
                left, right = grad[:, :hw], grad[:, hw:]
                mine = jnp.where(x == 0, left, right)
                theirs = jnp.where(x == 0, right, left)
                g = jnp.concatenate([mine, lax.ppermute(theirs, "dp", swap_x)], 1)
                got[cur] = {"g": g, "ups": [], "dns": []}
                st["ag"] = exchange(g, g, 0, n - 1)
            work(todo, ins, flat)
        for s in (0, 1):
            if state[s]["ag"]:
                got[streams[s][-1]]["ups"].append(state[s]["ag"][0])
                got[streams[s][-1]]["dns"].append(state[s]["ag"][1])
        for h in sorted(events):
            _, todo, ins, flat = half_slot(h, [])
            work(todo, ins, flat)
        ig, wg_out = out["ig"], out["wg"]
        acts = [acts[k] for k in range(count)]

        ig = ig.reshape(2, n, tb, depth)
        def over_x(v):
            return v[0] + lax.ppermute(v[1], "dp", swap_x)

        def over_y(v):
            if ncol != 2:
                return lax.psum_scatter(v, "col", scatter_dimension=v.ndim - 1, tiled=True)
            left, right = v[..., :half_d], v[..., half_d:]
            keep, give = jnp.where(y == 0, left, right), jnp.where(y == 0, right, left)
            return keep + lax.ppermute(give, "col", swap_y)

        mid = n // 2
        mine = jnp.concatenate([over_y(over_x(ig[:, :mid])), over_x(over_y(ig[:, mid:]))], 0)
        input_grad = unrotate(mine, z, n).reshape(tokens, -1)
        return jnp.concatenate(acts, 1), input_grad, wg_out

    return body


def solution(mesh):
    in_specs = (P("dp", ("row", "col")), P("row", "col"), P(("dp", "row"), "col"))
    out_specs = (P(("dp", "row"), "col"), P("dp", ("row", "col")), P("row", "col"))
    body = make_body(mesh.shape["row"], mesh.shape["col"])
    return jax.shard_map(body, mesh=mesh, in_specs=in_specs, out_specs=out_specs, check_vma=False)
```
